256 devices in a mesh: sample: 32 (over x, z_hi, core), tensor: 8 (over y, z_lo).
Axes of the slice: x: 4, y: 4, z: 8 (z_hi: 4, z_lo: 2; z = z_hi * 2 + z_lo), core: 2. Of those that a mesh axis runs over, the one named last changes fastest.
Arguments:
- prompt_x: bfloat16 [3072, 5120], P('sample'), may hold values from -6 to 6
- resp_x: bfloat16 [32, 256, 5120], P('sample'), may hold values from -6 to 6
- queries: bfloat16 [32, 256, 8192], P('sample', None, 'tensor'), may hold values from -8 to 8
- d_attn: bfloat16 [32, 256, 8192], P('sample', None, 'tensor'), may hold values from -6 to 6
- w_key: bfloat16 [5120, 1024], P(None, 'tensor'), may hold values from -0.078125 to 0.078125
- w_value: bfloat16 [5120, 1024], P(None, 'tensor'), may hold values from -0.078125 to 0.078125
- lengths: int32 [32], P('sample'), may hold values from 64 to 256, as said below
Outputs:
- d_queries: bfloat16 [32, 256, 8192], P('sample', None, 'tensor')
- d_resp_x: bfloat16 [32, 256, 5120], P('sample', None, 'tensor')
- d_prompt_x: bfloat16 [3072, 5120], P('sample', 'tensor')
- d_w_key: bfloat16 [5120, 1024], P('sample', 'tensor')
- d_w_value: bfloat16 [5120, 1024], P('sample', 'tensor')
The draws below stay inside these ranges and needn't reach their ends.
Inputs may be any that keep to these rules, and one draw needn't show every extreme that they name: `lengths`: some response has all 256 tokens valid.
All inputs are finite; a program needn't handle non-finite values.
Results may differ from the reference program's by a relative error of at most 0.015.
The reference program's roundings to bfloat16 on the way count: a program that leaves them out, or rounds other values in their place, can miss the bound.
Values may be sent and summed in bfloat16 or wider, within the bound.
A program may use at most 128 MiB of HBM per device.

```python
import jax
import jax.numpy as jnp
from jax import lax

D = 5120
HQ = 64
KVH = 8
HD = 128
RLEN = 256
RESPONSES = 32
PLEN = 3072


def draw_queries(key, part):
    key = jax.random.fold_in(key, 11)
    first = jax.random.fold_in(key, 0)
    result = jnp.clip(jax.random.normal(first, (RESPONSES, RLEN, HQ * HD), jnp.float32), -4.0, 4.0)
    return result.astype(jnp.bfloat16)


def draw_lengths(key, part):
    key = jax.random.fold_in(key, 5)
    first, second = jax.random.split(key)
    values = jax.random.randint(first, (RESPONSES,), RLEN // 4, RLEN + 1)
    full = jax.random.randint(second, (), 0, RESPONSES)
    return jnp.where(jnp.arange(RESPONSES) == full, RLEN, values).astype(jnp.int32)


def level_of(key, extent, shards, low, top_value):
    def one(dim, shards_of):
        heights = jax.random.uniform(jax.random.fold_in(jax.random.fold_in(key, 6), dim), (shards_of,), jnp.float32, low / len(shards), top_value / len(shards))
        return jnp.repeat(jnp.exp(heights), extent[dim] // shards_of).reshape((-1,) + (1,) * (len(extent) - dim - 1))

    gain = one(*shards[0])
    for cut in shards[1:]:
        gain = gain * one(*cut)
    return gain


def noise(key, dims, spread, bound, cuts=(), kind=jnp.bfloat16):
    array = spread * jax.random.normal(key, dims, jnp.float32)
    if cuts:
        array = array * level_of(key, dims, cuts, -0.22, 0.18)
    return jnp.clip(array, -bound, bound).astype(kind)


def setup_inputs(seed: int = 0) -> dict:
    arg_keys = jax.random.split(jax.random.key(seed), 8)
    prompt_x = noise(arg_keys[0], (PLEN, D), 1.0, 6.0, ((0, 32),))
    resp_x = noise(arg_keys[1], (RESPONSES, RLEN, D), 1.0, 6.0, ((0, 32),))
    queries = draw_queries(jax.random.fold_in(arg_keys[7], 71), 0)
    d_attn = noise(arg_keys[3], (RESPONSES, RLEN, HQ * HD), 1.0, 6.0, ((0, 32), (2, 8)))
    w_key = noise(arg_keys[4], (D, KVH * HD), D ** -0.5, 0.078125, ((1, 8),))
    w_value = noise(arg_keys[5], (D, KVH * HD), D ** -0.5, 0.078125, ((1, 8),))
    lengths = draw_lengths(jax.random.fold_in(arg_keys[7], 71), 0)
    return {"prompt_x": prompt_x, "resp_x": resp_x, "queries": queries, "d_attn": d_attn, "w_key": w_key, "w_value": w_value, "lengths": lengths}


def reference(prompt_x, resp_x, queries, d_attn, w_key, w_value, lengths):
    scale = HD ** -0.5
    group = HQ // KVH
    nk = PLEN + RLEN
    prompt_k = jnp.dot(prompt_x, w_key, preferred_element_type=jnp.float32).astype(jnp.bfloat16)
    prompt_v = jnp.dot(prompt_x, w_value, preferred_element_type=jnp.float32).astype(jnp.bfloat16)
    rows = jnp.arange(RLEN)[:, None]
    cols = jnp.arange(nk)[None, :]
    allowed = (cols < PLEN) | (cols - PLEN <= rows)

    def one_response(carry, item):
        hidden, query, grad, length = item
        resp_k = jnp.dot(hidden, w_key, preferred_element_type=jnp.float32).astype(jnp.bfloat16)
        resp_v = jnp.dot(hidden, w_value, preferred_element_type=jnp.float32).astype(jnp.bfloat16)
        keys = jnp.concatenate([prompt_k, resp_k], 0).reshape(nk, KVH, HD).astype(jnp.float32)
        values = jnp.concatenate([prompt_v, resp_v], 0).reshape(nk, KVH, HD).astype(jnp.float32)
        qry = query.reshape(RLEN, KVH, group, HD).astype(jnp.float32)
        valid = jnp.arange(RLEN) < length
        gout = jnp.where(valid[:, None], grad, jnp.zeros_like(grad)).reshape(RLEN, KVH, group, HD).astype(jnp.float32)
        scores = jnp.einsum('ikgd,jkd->kgij', qry, keys) * scale
        scores = jnp.where(allowed, scores, -jnp.inf)
        top = jnp.max(scores, axis=-1, keepdims=True)
        expo = jnp.exp(scores - top)
        probs = expo / jnp.sum(expo, axis=-1, keepdims=True)
        probs_low = probs.astype(jnp.bfloat16).astype(jnp.float32)
        out = jnp.einsum('kgij,jkd->ikgd', probs_low, values)
        row_dot = jnp.einsum('ikgd,ikgd->kgi', gout, out)
        grad_probs = jnp.einsum('ikgd,jkd->kgij', gout, values)
        grad_scores = (probs * (grad_probs - row_dot[..., None])).astype(jnp.bfloat16).astype(jnp.float32)
        dq = (jnp.einsum('kgij,jkd->ikgd', grad_scores, keys) * scale).astype(jnp.bfloat16)
        gk = jnp.einsum('kgij,ikgd->jkd', grad_scores, qry).reshape(nk, KVH * HD) * scale
        gv = jnp.einsum('kgij,ikgd->jkd', probs_low, gout).reshape(nk, KVH * HD)
        resp_gk = gk[PLEN:].astype(jnp.bfloat16)
        resp_gv = gv[PLEN:].astype(jnp.bfloat16)
        dx = jnp.dot(resp_gk, w_key.T, preferred_element_type=jnp.float32) + jnp.dot(resp_gv, w_value.T, preferred_element_type=jnp.float32)
        sum_pk, sum_pv, sum_wk, sum_wv = carry
        sum_pk = sum_pk + gk[:PLEN]
        sum_pv = sum_pv + gv[:PLEN]
        sum_wk = sum_wk + jnp.dot(hidden.T, resp_gk, preferred_element_type=jnp.float32)
        sum_wv = sum_wv + jnp.dot(hidden.T, resp_gv, preferred_element_type=jnp.float32)
        return (sum_pk, sum_pv, sum_wk, sum_wv), (dq.reshape(RLEN, HQ * HD), dx.astype(jnp.bfloat16))

    start = (jnp.zeros((PLEN, KVH * HD), jnp.float32), jnp.zeros((PLEN, KVH * HD), jnp.float32),
             jnp.zeros((D, KVH * HD), jnp.float32), jnp.zeros((D, KVH * HD), jnp.float32))
    (sum_pk, sum_pv, sum_wk, sum_wv), (d_queries, d_resp_x) = lax.scan(one_response, start, (resp_x, queries, d_attn, lengths))
    prompt_gk = sum_pk.astype(jnp.bfloat16)
    prompt_gv = sum_pv.astype(jnp.bfloat16)
    d_prompt_x = (jnp.dot(prompt_gk, w_key.T, preferred_element_type=jnp.float32) + jnp.dot(prompt_gv, w_value.T, preferred_element_type=jnp.float32)).astype(jnp.bfloat16)
    d_w_key = (sum_wk + jnp.dot(prompt_x.T, prompt_gk, preferred_element_type=jnp.float32)).astype(jnp.bfloat16)
    d_w_value = (sum_wv + jnp.dot(prompt_x.T, prompt_gv, preferred_element_type=jnp.float32)).astype(jnp.bfloat16)
    return (d_queries, d_resp_x, d_prompt_x, d_w_key, d_w_value)
```

```python
import functools
import math

import jax
import jax.numpy as jnp
from jax import lax
from jax.experimental import pallas as pl
from jax.experimental.pallas import tpu as pltpu
from jax.sharding import PartitionSpec as P

f32 = jnp.float32
bf16 = jnp.bfloat16
MESH = pl.DeviceIdType.MESH
HD = 128
HEADS = 8
RL = 256
NX, NZ, NC, NY, NL = 4, 4, 2, 4, 2
NT = NY * NL
PR = 96
BLK = NZ * NC * PR
NP = NX * BLK
DM = 5120
DR = DM // (NX * NZ * NC)
DT = DM // NT
SCALE = HD**-0.5
SCALE2 = SCALE * math.log2(math.e)


def dot(a, b):
    return lax.dot_general(a, b, (((1,), (0,)), ((), ())), preferred_element_type=f32)


def dot_t(a, b):
    return lax.dot_general(a, b, (((1,), (1,)), ((), ())), preferred_element_type=f32)


def offset(k):
    return k + k // 2 - 2 * (k // 3)


def kernel(
    px_hbm, rx_hbm, q_hbm, g_hbm, wk_hbm, wv_hbm, len_ref,
    dq_hbm, drx_hbm, dpx_hbm, dwk_hbm, dwv_hbm,
    px, rx, q_in, g_in, w, rxt, pxt,
    kv, kvt, qa, ga, qt, gt,
    e_ref, er_ref, gs_ref, s_ref, mc_ref, m_ref, mm, ll, oo, al_ref, be_ref, rd, dqt,
    gblk, keep, rcs, rcr, rxs, rxr, rzs, rzr, zacc,
    rg_all, pg_all, wsl, dwr, dkeep, dcs, dcr, dxs, dxr, dzs, dzr,
    dq_out, drx_out, dpx_out, dw_out,
    ld_sem, out_sem,
    agz_s, agz_r, agx_s, agx_r, agc_s, agc_r,
    w_s, w_r, wc_s, wc_r, t_s, t_r,
    rc_s, rc_r, rx_s, rx_r, rz_s, rz_r, p_s, p_r,
    dc_s, dc_r, dx_s, dx_r, dz_s, dz_r,
):
    sm = lax.axis_index("sample")
    tn = lax.axis_index("tensor")
    c = lax.rem(sm, NC)
    z = lax.rem(sm // NC, NZ)
    x = sm // (NC * NZ)
    y = tn // NL
    lo = lax.rem(tn, NL)
    oc = 1 - c

    def dev_s(xx, zz, cc):
        return ((xx * NZ + zz) * NC + cc, tn)

    core = dev_s(x, z, oc)

    def dev_x(o):
        return dev_s(lax.rem(x + o, NX), z, c)

    def dev_z(o):
        return dev_s(x, lax.rem(z + o, NZ), c)

    def dev_t(o):
        return (sm, lax.rem(tn + o, NT))

    def dev_y(o):
        return (sm, lax.rem(y + o, NY) * NL + lo)

    dev_l = (sm, y * NL + 1 - lo)

    def remote(src, dst, ss, rs, dev):
        return pltpu.make_async_remote_copy(
            src_ref=src, dst_ref=dst, send_sem=ss, recv_sem=rs, device_id=dev,
            device_id_type=MESH,
        )

    def al(v, n):
        return pl.multiple_of(v, n)

    loads = [
        pltpu.make_async_copy(px_hbm, px, ld_sem.at[0]),
        pltpu.make_async_copy(wk_hbm, w.at[:, pl.ds(0, HD)], ld_sem.at[1]),
        pltpu.make_async_copy(wv_hbm, w.at[:, pl.ds(HD, HD)], ld_sem.at[2]),
        pltpu.make_async_copy(rx_hbm.at[0], rx, ld_sem.at[3]),
        pltpu.make_async_copy(q_hbm.at[0], q_in, ld_sem.at[4]),
        pltpu.make_async_copy(g_hbm.at[0], g_in, ld_sem.at[5]),
    ]
    for cp in loads:
        cp.start()

    barrier = pltpu.get_barrier_semaphore()
    peers = [core] + [dev_x(o) for o in (1, 2, 3)] + [dev_z(o) for o in (1, 2, 3)]
    peers += [dev_t(o) for o in range(1, NT)]
    for dev in peers:
        pl.semaphore_signal(barrier, inc=1, device_id=dev, device_id_type=MESH)

    loads[0].wait()
    loads[1].wait()
    loads[2].wait()

    def chunk(xx, zz, cc):
        return pl.ds(al(((xx * NZ + zz) * NC + cc) * PR, PR), PR)

    kv[chunk(x, z, c), :] = dot(px[...], w[...]).astype(bf16)
    pl.semaphore_wait(barrier, len(peers))

    def ag_z(i):
        rows = chunk(x, z, c)
        return remote(kv.at[rows, :], kv.at[rows, :], agz_s.at[i], agz_r.at[i], dev_z(i + 1))

    def ag_x(j, i):
        rows = chunk(x, lax.rem(z - j + NZ, NZ), c)
        return remote(
            kv.at[rows, :], kv.at[rows, :], agx_s.at[i, j], agx_r.at[i, j],
            dev_x(offset(i + 1)),
        )

    def ag_c(k, j):
        rows = chunk(lax.rem(x - offset(k) + NX, NX), lax.rem(z - j + NZ, NZ), c)
        return remote(kv.at[rows, :], kv.at[rows, :], agc_s.at[k, j], agc_r.at[k, j], core)

    for i in range(3):
        ag_z(i).start()
    for i in range(3):
        ag_x(0, i).start()
    ag_c(0, 0).start()

    loads[3].wait()
    kv[NP : NP + RL, :] = dot(rx[...], w[...]).astype(bf16)
    loads[4].wait()
    loads[5].wait()
    valid = lax.broadcasted_iota(jnp.int32, (RL, HD), 0) < len_ref[0]
    for h in range(HEADS):
        qh = q_in[:, h * HD : (h + 1) * HD]
        gh = jnp.where(valid, g_in[:, h * HD : (h + 1) * HD], jnp.zeros((RL, HD), bf16))
        qa[h * RL : (h + 1) * RL, :] = qh
        ga[h * RL : (h + 1) * RL, :] = gh
        qt[h] = qh.T
        gt[h] = gh.T
    kvt[NX, :, 0:RL] = kv[NP : NP + RL, :].T

    for j in range(1, NZ):
        ag_z(j - 1).wait_recv()
        for i in range(3):
            ag_x(j, i).start()
        ag_c(0, j).start()

    def hc(h):
        return slice(h * RL, (h + 1) * RL)

    def scores(base, n, h, first):
        s = dot(kv[pl.ds(base, n), 0:HD], qt[h])
        if first:
            ri = lax.broadcasted_iota(jnp.int32, (RL, RL), 0)
            ci = lax.broadcasted_iota(jnp.int32, (RL, RL), 1)
            s = jnp.where(ri <= ci, s, -jnp.inf)
        s_ref[h % 2, 0:n, :] = s
        mc_ref[h % 2] = jnp.max(s, axis=0, keepdims=True) * SCALE2

    def expo(slot, n, h, first):
        mc = mc_ref[h % 2]
        e = jnp.exp2(s_ref[h % 2, 0:n, :] * SCALE2 - mc)
        lc = jnp.sum(e, axis=0, keepdims=True)
        if first:
            er_ref[:, hc(h)] = e.astype(bf16)
        else:
            e_ref[slot, :, hc(h)] = e.astype(bf16)
        m_ref[slot, h] = mc
        if first:
            mm[h] = mc
            ll[h] = lc
        else:
            mo = mm[h]
            mn = jnp.maximum(mo, mc)
            a = jnp.exp2(mo - mn)
            b = jnp.exp2(mc - mn)
            mm[h] = mn
            ll[h] = ll[h] * a + lc * b
            al_ref[h] = a
            be_ref[h] = b

    def outs(slot, n, h, first):
        e = er_ref[:, hc(h)] if first else e_ref[slot, :, hc(h)]
        o = dot(kvt[slot, HD : 2 * HD, 0:n], e)
        oo[h] = o if first else oo[h] * al_ref[h] + o * be_ref[h]

    def pass1(slot, base, n, first):
        scores(base, n, 0, first)
        for h in range(HEADS):
            if h < HEADS - 1:
                scores(base, n, h + 1, first)
            expo(slot, n, h, first)
            if h:
                outs(slot, n, h - 1, first)
        outs(slot, n, HEADS - 1, first)

    pass1(NX, NP, RL, True)

    def block_of(k):
        return al(lax.rem(x - offset(k) + NX, NX) * BLK, BLK)

    def blocks1(k, _):
        @pl.when(k < NX - 1)
        def _():
            for j in range(NZ):
                ag_x(j, k).wait_recv()
                ag_c(k + 1, j).start()

        for j in range(NZ):
            ag_c(k, j).wait_recv()
        base = block_of(k)
        kvt[k] = kv[pl.ds(base, BLK), :].T
        pass1(k, base, BLK, False)
        return 0

    lax.fori_loop(0, NX, blocks1, 0)

    def w_send(o):
        t2 = lax.rem(tn + o, NT)
        src = w.at[pl.ds(al(t2 * DT + c * (DT // 2), DT // 2), DT // 2), :]
        dst = wsl.at[tn, pl.ds(al(c * (DT // 2), DT // 2), DT // 2), :]
        return remote(src, dst, w_s.at[o - 1], w_r.at[o - 1], dev_t(o))

    def w_core(o):
        ref = wsl.at[
            lax.rem(tn - o + NT, NT), pl.ds(al(c * (DT // 2), DT // 2), DT // 2), :
        ]
        return remote(ref, ref, wc_s.at[o - 1], wc_r.at[o - 1], core)

    for o in range(1, NT):
        w_send(o).start()

    for h in range(HEADS):
        rl = 1.0 / ll[h]
        rd[h] = jnp.sum(gt[h].astype(f32) * (oo[h] * rl), axis=0, keepdims=True)
        ll[h] = rl
        dqt[h] = jnp.zeros((HD, RL), f32)

    def grads(base, n, h):
        s_ref[h % 2, 0:n, :] = dot(kv[pl.ds(base, n), HD : 2 * HD], gt[h])

    def gscores(slot, n, h, first):
        fac = jnp.exp2(m_ref[slot, h] - mm[h]) * ll[h]
        e = er_ref[:, hc(h)] if first else e_ref[slot, :, hc(h)]
        p = e.astype(f32) * fac
        pb = p.astype(bf16)
        if first:
            er_ref[:, hc(h)] = pb
        else:
            e_ref[slot, :, hc(h)] = pb
        gs_ref[0:n, hc(h)] = (p * (s_ref[h % 2, 0:n, :] - rd[h])).astype(bf16)

    def dqs(slot, n, h):
        dqt[h] += dot(kvt[slot, 0:HD, 0:n], gs_ref[0:n, hc(h)])

    def pass2(slot, base, n, first, heads=range(HEADS)):
        grads(base, n, heads[0])
        for h in heads:
            if h < heads[-1]:
                grads(base, n, h + 1)
            gscores(slot, n, h, first)
            if h > heads[0]:
                dqs(slot, n, h - 1)
        dqs(slot, n, heads[-1])

    def key_grads(slot, n, first):
        pb = er_ref[...] if first else e_ref[slot]
        gblk[0:n, 0:HD] = dot(gs_ref[0:n, :], qa[...]) * SCALE
        gblk[0:n, HD : 2 * HD] = dot(pb, ga[...])

    pass2(NX, NP, RL, True)
    key_grads(NX, RL, True)
    rg_all[tn] = gblk[0:RL, :].astype(bf16)

    def t_own(i):
        ref = rg_all.at[tn]
        return remote(ref, ref, t_s.at[i], t_r.at[i], dev_l if i == 0 else dev_y(i))

    def t_fwd(i):
        ref = rg_all.at[y * NL + 1 - lo]
        return remote(ref, ref, t_s.at[3 + i], t_r.at[3 + i], dev_y(i))

    for i in range(4):
        t_own(i).start()

    def rs_c(k):
        return remote(rcs.at[k], rcr.at[k], rc_s.at[k], rc_r.at[k], core)

    def rs_x(k):
        return remote(rxs.at[k], rxr.at[k], rx_s.at[k], rx_r.at[k], dev_x(NX - offset(NX - 1 - k)))

    def rs_z(i):
        return remote(rzs.at[i], rzr.at[i], rz_s.at[i], rz_r.at[i], dev_z(i + 1))

    def blocks2(k, _):
        slot = NX - 1 - k
        base = block_of(slot)
        pass2(slot, base, BLK, False, range(0, HEADS // 2))

        @pl.when(k > 0)
        def _():
            rs_c(k - 1).wait_recv()
            for zz in range(NZ):
                rxs[k - 1, zz] = (keep[k - 1, zz] + rcr[k - 1, zz].astype(f32)).astype(bf16)
            rs_x(k - 1).start()

        pass2(slot, base, BLK, False, range(HEADS // 2, HEADS))
        key_grads(slot, BLK, False)
        for zz in range(NZ):
            rcs[k, zz] = gblk[pl.ds(al((zz * NC + oc) * PR, PR), PR), :].astype(bf16)
            keep[k, zz] = gblk[pl.ds(al((zz * NC + c) * PR, PR), PR), :]
        rs_c(k).start()

        @pl.when(k == 1)
        def _():
            t_own(0).wait_recv()
            for i in range(1, 4):
                t_fwd(i).start()

        return 0

    lax.fori_loop(0, NX, blocks2, 0)

    for h in range(HEADS):
        dq_out[:, h * HD : (h + 1) * HD] = (dqt[h].T * SCALE).astype(bf16)
    out_dq = pltpu.make_async_copy(dq_out, dq_hbm.at[0], out_sem.at[0])
    out_dq.start()

    rs_c(NX - 1).wait_recv()
    for k in range(NX - 1):
        rs_x(k).wait_recv()
    for zz in range(NZ):
        tot = keep[NX - 1, zz] + rcr[NX - 1, zz].astype(f32)
        for k in range(NX - 1):
            tot = tot + rxr[k, zz].astype(f32)
        zacc[zz] = tot
    for i in range(3):
        rzs[i] = zacc[lax.rem(z + i + 1, NZ)].astype(bf16)
        rs_z(i).start()

    for o in range(1, NT):
        w_send(o).wait_recv()
        w_core(o).start()
    wsl[tn] = w[pl.ds(al(tn * DT, DT), DT), :]
    pxt[...] = px[...].T
    rxt[...] = rx[...].T
    own_rg = rg_all[tn]
    for i in range(NX):
        rows = slice(i * (DM // NX), (i + 1) * (DM // NX))
        dwr[rows, :] = dot(rxt[rows, :], own_rg)

    for i in range(3):
        rs_z(i).wait_recv()
    tot = zacc[z]
    for i in range(3):
        tot = tot + rzr[i].astype(f32)
    pg = tot.astype(bf16)
    pg_all[tn] = pg

    def p_send(o):
        return remote(pg_all.at[tn], pg_all.at[tn], p_s.at[o - 1], p_r.at[o - 1], dev_t(o))

    def dw_c(g):
        return remote(dcs.at[g], dcr.at[g], dc_s.at[g], dc_r.at[g], core)

    def dw_x(g, i):
        return remote(
            dxs.at[g, i], dxr.at[g, i], dx_s.at[g, i], dx_r.at[g, i], dev_x(offset(3 - i))
        )

    def dw_z(g):
        return remote(dzs.at[g], dzr.at[g], dz_s.at[g], dz_r.at[g], dev_z(offset(3 - g)))

    def dw_group(g, _):
        zz = lax.rem(z + offset(3 - g), NZ)
        for i in range(NX):
            xx = lax.rem(x + offset(3 - i), NX)
            first = (xx * NZ + zz) * NC
            theirs = pl.ds(al((first + oc) * DR, DR), DR)
            mine = pl.ds(al((first + c) * DR, DR), DR)
            dcs[g, i] = (dwr[theirs, :] + dot(pxt[theirs, :], pg)).astype(bf16)
            dkeep[g, i] = dwr[mine, :] + dot(pxt[mine, :], pg)
        dw_c(g).start()
        return 0

    lax.fori_loop(0, NZ, dw_group, 0)
    for o in range(1, NT):
        p_send(o).start()

    def dw_sum(g, _):
        dw_c(g).wait_recv()
        for i in range(NX - 1):
            dxs[g, i] = (dkeep[g, i] + dcr[g, i].astype(f32)).astype(bf16)
            dw_x(g, i).start()
        dkeep[g, NX - 1] = dkeep[g, NX - 1] + dcr[g, NX - 1].astype(f32)
        return 0

    lax.fori_loop(0, NZ, dw_sum, 0)

    for i in range(1, 4):
        t_own(i).wait_recv()
        t_fwd(i).wait_recv()
    for o in range(1, NT):
        w_core(o).wait_recv()
    acc = dot_t(rg_all[0], wsl[0])
    for t2 in range(1, NT):
        acc = acc + dot_t(rg_all[t2], wsl[t2])
    drx_out[...] = acc.astype(bf16)
    out_drx = pltpu.make_async_copy(drx_out, drx_hbm.at[0], out_sem.at[1])
    out_drx.start()

    def dw_last(g, _):
        for i in range(NX - 1):
            dw_x(g, i).wait_recv()
        tot = dkeep[g, NX - 1]
        for i in range(NX - 1):
            tot = tot + dxr[g, i].astype(f32)
        dkeep[g, NX - 1] = tot

        @pl.when(g < NZ - 1)
        def _():
            dzs[g] = tot.astype(bf16)
            dw_z(g).start()

        return 0

    lax.fori_loop(0, NZ, dw_last, 0)

    for o in range(1, NT):
        p_send(o).wait_recv()
    acc = dot_t(pg_all[0], wsl[0])
    for t2 in range(1, NT):
        acc = acc + dot_t(pg_all[t2], wsl[t2])
    dpx_out[...] = acc.astype(bf16)
    out_dpx = pltpu.make_async_copy(dpx_out, dpx_hbm, out_sem.at[2])
    out_dpx.start()

    for g in range(NZ - 1):
        dw_z(g).wait_recv()
    tot = dkeep[NZ - 1, NX - 1]
    for g in range(NZ - 1):
        tot = tot + dzr[g].astype(f32)
    dw_out[0] = tot[:, 0:HD].astype(bf16)
    dw_out[1] = tot[:, HD : 2 * HD].astype(bf16)
    out_dwk = pltpu.make_async_copy(dw_out.at[0], dwk_hbm, out_sem.at[3])
    out_dwv = pltpu.make_async_copy(dw_out.at[1], dwv_hbm, out_sem.at[4])
    out_dwk.start()
    out_dwv.start()

    for i in range(3):
        ag_z(i).wait_send()
        for j in range(NZ):
            ag_x(j, i).wait_send()
        rs_x(i).wait_send()
        rs_z(i).wait_send()
        dw_z(i).wait_send()
    for k in range(NX):
        for j in range(NZ):
            ag_c(k, j).wait_send()
        rs_c(k).wait_send()
        dw_c(k).wait_send()
        for i in range(NX - 1):
            dw_x(k, i).wait_send()
    for o in range(1, NT):
        w_send(o).wait_send()
        w_core(o).wait_send()
        p_send(o).wait_send()
    for i in range(4):
        t_own(i).wait_send()
    for i in range(1, 4):
        t_fwd(i).wait_send()
    for cp in (out_dq, out_drx, out_dpx, out_dwk, out_dwv):
        cp.wait()


def local(prompt_x, resp_x, queries, d_attn, w_key, w_value, lengths):
    any_ = pl.BlockSpec(memory_space=pl.ANY)
    v = pltpu.VMEM
    dma = pltpu.SemaphoreType.DMA
    scratch = [
        v((PR, DM), bf16), v((RL, DM), bf16), v((RL, HEADS * HD), bf16), v((RL, HEADS * HD), bf16),
        v((DM, 2 * HD), bf16), v((DM, RL), bf16), v((DM, PR), bf16),
        v((NP + RL, 2 * HD), bf16), v((NX + 1, 2 * HD, BLK), bf16),
        v((HEADS * RL, HD), bf16), v((HEADS * RL, HD), bf16),
        v((HEADS, HD, RL), bf16), v((HEADS, HD, RL), bf16),
        v((NX, BLK, HEADS * RL), bf16), v((RL, HEADS * RL), bf16), v((BLK, HEADS * RL), bf16),
        v((2, BLK, RL), f32), v((2, 1, RL), f32), v((NX + 1, HEADS, 1, RL), f32),
        v((HEADS, 1, RL), f32), v((HEADS, 1, RL), f32), v((HEADS, HD, RL), f32),
        v((HEADS, 1, RL), f32), v((HEADS, 1, RL), f32), v((HEADS, 1, RL), f32),
        v((HEADS, HD, RL), f32),
        v((BLK, 2 * HD), f32), v((NX, NZ, PR, 2 * HD), f32),
        v((NX, NZ, PR, 2 * HD), bf16), v((NX, NZ, PR, 2 * HD), bf16),
        v((3, NZ, PR, 2 * HD), bf16), v((3, NZ, PR, 2 * HD), bf16),
        v((3, PR, 2 * HD), bf16), v((3, PR, 2 * HD), bf16), v((NZ, PR, 2 * HD), f32),
        v((NT, RL, 2 * HD), bf16), v((NT, PR, 2 * HD), bf16), v((NT, DT, 2 * HD), bf16),
        v((DM, 2 * HD), f32), v((NZ, NX, DR, 2 * HD), f32),
        v((NZ, NX, DR, 2 * HD), bf16), v((NZ, NX, DR, 2 * HD), bf16),
        v((NZ, NX - 1, DR, 2 * HD), bf16), v((NZ, NX - 1, DR, 2 * HD), bf16),
        v((NZ - 1, DR, 2 * HD), bf16), v((NZ - 1, DR, 2 * HD), bf16),
        v((RL, HEADS * HD), bf16), v((RL, DT), bf16), v((PR, DT), bf16), v((2, DR, HD), bf16),
        dma((6,)), dma((5,)),
        dma((3,)), dma((3,)), dma((3, NZ)), dma((3, NZ)), dma((NX, NZ)), dma((NX, NZ)),
        dma((NT - 1,)), dma((NT - 1,)), dma((NT - 1,)), dma((NT - 1,)),
        dma((NT - 1,)), dma((NT - 1,)),
        dma((NX,)), dma((NX,)), dma((3,)), dma((3,)), dma((3,)), dma((3,)),
        dma((NT - 1,)), dma((NT - 1,)),
        dma((NZ,)), dma((NZ,)), dma((NZ, 3)), dma((NZ, 3)), dma((3,)), dma((3,)),
    ]
    return pl.pallas_call(
        kernel,
        out_shape=(
            jax.ShapeDtypeStruct((1, RL, HEADS * HD), bf16),
            jax.ShapeDtypeStruct((1, RL, DT), bf16),
            jax.ShapeDtypeStruct((PR, DT), bf16),
            jax.ShapeDtypeStruct((DR, HD), bf16),
            jax.ShapeDtypeStruct((DR, HD), bf16),
        ),
        in_specs=[any_] * 6 + [pl.BlockSpec(memory_space=pltpu.SMEM)],
        out_specs=(any_,) * 5,
        scratch_shapes=scratch,
        compiler_params=pltpu.CompilerParams(
            collective_id=0, has_side_effects=True, vmem_limit_bytes=63 * 2**20
        ),
        name="kv_backward",
    )(prompt_x, resp_x, queries, d_attn, w_key, w_value, lengths)


def solution(mesh):
    placed = (
        P("sample", None),
        P("sample", None, None),
        P("sample", None, "tensor"),
        P("sample", None, "tensor"),
        P(None, "tensor"),
        P(None, "tensor"),
        P("sample"),
    )
    return jax.shard_map(
        local,
        mesh=mesh,
        in_specs=placed,
        out_specs=(
            P("sample", None, "tensor"),
            P("sample", None, "tensor"),
            P("sample", "tensor"),
            P("sample", "tensor"),
            P("sample", "tensor"),
        ),
        check_vma=False,
    )
```

```python
import functools
import math

import jax
import jax.numpy as jnp
from jax import lax
from jax.experimental import pallas as pl
from jax.experimental.pallas import tpu as pltpu
from jax.sharding import PartitionSpec as P

f32 = jnp.float32
bf16 = jnp.bfloat16
MESH = pl.DeviceIdType.MESH
HD = 128
HEADS = 8
RL = 256
NX, NZ, NC, NY, NL = 4, 4, 2, 4, 2
NT = NY * NL
PR = 96
BLK = NX * NC * PR
NP = NZ * BLK
DM = 5120
DR = DM // (NX * NZ * NC)
DT = DM // NT
SCALE = HD**-0.5
SCALE2 = SCALE * math.log2(math.e)


def dot(a, b):
    return lax.dot_general(a, b, (((1,), (0,)), ((), ())), preferred_element_type=f32)


def dot_t(a, b):
    return lax.dot_general(a, b, (((1,), (1,)), ((), ())), preferred_element_type=f32)


def offset(k):
    return k + k // 2 - 2 * (k // 3)


def kernel(
    px_hbm, rx_hbm, q_hbm, g_hbm, wk_hbm, wv_hbm, len_ref,
    dq_hbm, drx_hbm, dpx_hbm, dwk_hbm, dwv_hbm,
    px, rx, q_in, g_in, w, rxt, pxt,
    kv, kvt, qa, ga, qt, gt,
    e_ref, er_ref, gs_ref, s_ref, mc_ref, m_ref, mm, ll, oo, al_ref, be_ref, rd, dqt,
    gblk, keep, rcs, rcr, rxs, rxr, rzs, rzr,
    rg_all, pg_all, wsl, dwr, dkeep, dcs, dcr, dxs, dxr, dzs, dzr,
    dq_out, drx_out, dpx_out, dw_out,
    ld_sem, out_sem,
    agz_s, agz_r, agx_s, agx_r, agc_s, agc_r,
    w_s, w_r, wc_s, wc_r, t_s, t_r,
    rc_s, rc_r, rx_s, rx_r, rz_s, rz_r, p_s, p_r,
    dc_s, dc_r, dx_s, dx_r, dz_s, dz_r,
):
    sm = lax.axis_index("sample")
    tn = lax.axis_index("tensor")
    c = lax.rem(sm, NC)
    z = lax.rem(sm // NC, NZ)
    x = sm // (NC * NZ)
    y = tn // NL
    lo = lax.rem(tn, NL)
    oc = 1 - c

    def dev_s(xx, zz, cc):
        return ((xx * NZ + zz) * NC + cc, tn)

    core = dev_s(x, z, oc)

    def dev_x(o):
        return dev_s(lax.rem(x + o, NX), z, c)

    def dev_z(o):
        return dev_s(x, lax.rem(z + o, NZ), c)

    def dev_t(o):
        return (sm, lax.rem(tn + o, NT))

    def dev_y(o):
        return (sm, lax.rem(y + o, NY) * NL + lo)

    dev_l = (sm, y * NL + 1 - lo)

    def remote(src, dst, ss, rs, dev):
        return pltpu.make_async_remote_copy(
            src_ref=src, dst_ref=dst, send_sem=ss, recv_sem=rs, device_id=dev,
            device_id_type=MESH,
        )

    def al(v, n):
        return pl.multiple_of(v, n)

    loads = [
        pltpu.make_async_copy(px_hbm, px, ld_sem.at[0]),
        pltpu.make_async_copy(wk_hbm, w.at[:, pl.ds(0, HD)], ld_sem.at[1]),
        pltpu.make_async_copy(wv_hbm, w.at[:, pl.ds(HD, HD)], ld_sem.at[2]),
        pltpu.make_async_copy(rx_hbm.at[0], rx, ld_sem.at[3]),
        pltpu.make_async_copy(q_hbm.at[0], q_in, ld_sem.at[4]),
        pltpu.make_async_copy(g_hbm.at[0], g_in, ld_sem.at[5]),
    ]
    for cp in loads:
        cp.start()

    barrier = pltpu.get_barrier_semaphore()
    peers = [core] + [dev_x(o) for o in (1, 2, 3)] + [dev_z(o) for o in (1, 2, 3)]
    peers += [dev_t(o) for o in range(1, NT)]
    for dev in peers:
        pl.semaphore_signal(barrier, inc=1, device_id=dev, device_id_type=MESH)

    loads[0].wait()
    loads[1].wait()
    loads[2].wait()

    def chunk(xx, zz, cc):
        return pl.ds(al(((zz * NX + xx) * NC + cc) * PR, PR), PR)

    kv[chunk(x, z, c), :] = dot(px[...], w[...]).astype(bf16)
    pl.semaphore_wait(barrier, len(peers))

    def ag_z(i):
        rows = chunk(x, z, c)
        return remote(kv.at[rows, :], kv.at[rows, :], agz_s.at[i], agz_r.at[i], dev_z(i + 1))

    def ag_x(j, i):
        rows = chunk(x, lax.rem(z - j + NZ, NZ), c)
        return remote(
            kv.at[rows, :], kv.at[rows, :], agx_s.at[i, j], agx_r.at[i, j],
            dev_x(offset(i + 1)),
        )

    def ag_c(k, j):
        rows = chunk(lax.rem(x - offset(k) + NX, NX), lax.rem(z - j + NZ, NZ), c)
        return remote(kv.at[rows, :], kv.at[rows, :], agc_s.at[k, j], agc_r.at[k, j], core)

    for i in (1, 0, 2):
        ag_z(i).start()
    for i in (2, 0, 1):
        ag_x(0, i).start()
    ag_c(0, 0).start()

    def w_send(o):
        t2 = lax.rem(tn + o, NT)
        src = w.at[pl.ds(al(t2 * DT + c * (DT // 2), DT // 2), DT // 2), :]
        dst = wsl.at[tn, pl.ds(al(c * (DT // 2), DT // 2), DT // 2), :]
        return remote(src, dst, w_s.at[o - 1], w_r.at[o - 1], dev_t(o))

    def w_core(o):
        ref = wsl.at[
            lax.rem(tn - o + NT, NT), pl.ds(al(c * (DT // 2), DT // 2), DT // 2), :
        ]
        return remote(ref, ref, wc_s.at[o - 1], wc_r.at[o - 1], core)

    for o in (4, 2, 6):
        w_send(o).start()

    loads[3].wait()
    kv[NP : NP + RL, :] = dot(rx[...], w[...]).astype(bf16)
    loads[4].wait()
    loads[5].wait()
    valid = lax.broadcasted_iota(jnp.int32, (RL, HD), 0) < len_ref[0]
    for h in range(HEADS):
        qh = q_in[:, h * HD : (h + 1) * HD]
        gh = jnp.where(valid, g_in[:, h * HD : (h + 1) * HD], jnp.zeros((RL, HD), bf16))
        qa[h * RL : (h + 1) * RL, :] = qh
        ga[h * RL : (h + 1) * RL, :] = gh
        qt[h] = qh.T
        gt[h] = gh.T
    kvt[NX, :, 0:RL] = kv[NP : NP + RL, :].T

    def hc(h):
        return slice(h * RL, (h + 1) * RL)

    def scores(base, n, h, first):
        s = dot(kv[pl.ds(base, n), 0:HD], qt[h])
        if first:
            ri = lax.broadcasted_iota(jnp.int32, (RL, RL), 0)
            ci = lax.broadcasted_iota(jnp.int32, (RL, RL), 1)
            s = jnp.where(ri <= ci, s, -jnp.inf)
        s_ref[h % 2, 0:n, :] = s
        mc_ref[h % 2] = jnp.max(s, axis=0, keepdims=True) * SCALE2

    def expo(slot, n, h, first):
        mc = mc_ref[h % 2]
        e = jnp.exp2(s_ref[h % 2, 0:n, :] * SCALE2 - mc)
        lc = jnp.sum(e, axis=0, keepdims=True)
        if first:
            er_ref[:, hc(h)] = e.astype(bf16)
        else:
            e_ref[slot, :, hc(h)] = e.astype(bf16)
        m_ref[slot, h] = mc
        if first:
            mm[h] = mc
            ll[h] = lc
        else:
            mo = mm[h]
            mn = jnp.maximum(mo, mc)
            a = jnp.exp2(mo - mn)
            b = jnp.exp2(mc - mn)
            mm[h] = mn
            ll[h] = ll[h] * a + lc * b
            al_ref[h] = a
            be_ref[h] = b

    def outs(slot, n, h, first):
        e = er_ref[:, hc(h)] if first else e_ref[slot, :, hc(h)]
        o = dot(kvt[slot, HD : 2 * HD, 0:n], e)
        oo[h] = o if first else oo[h] * al_ref[h] + o * be_ref[h]

    def pass1(slot, base, n, first):
        scores(base, n, 0, first)
        for h in range(HEADS):
            if h < HEADS - 1:
                scores(base, n, h + 1, first)
            expo(slot, n, h, first)
            if h:
                outs(slot, n, h - 1, first)
        outs(slot, n, HEADS - 1, first)

    pass1(NX, NP, RL, True)

    def along_x(j):
        ag_z(j - 1).wait_recv()
        for i in (2, 0, 1):
            ag_x(j, i).start()
        ag_c(0, j).start()

    def across(j):
        for k in (1, 2, 3):
            ag_x(j, k - 1).wait_recv()
            ag_c(k, j).start()

    along_x(1)
    along_x(3)
    across(0)
    along_x(2)
    for o in (3, 5, 1, 7):
        w_send(o).start()

    def block_of(k):
        return al(lax.rem(z - offset(k) + NZ, NZ) * BLK, BLK)

    def blocks1(k, _):
        for i in range(NX):
            ag_c(i, offset(k)).wait_recv()
        base = block_of(k)
        kvt[k] = kv[pl.ds(base, BLK), :].T
        pass1(k, base, BLK, False)

        @pl.when(k == 0)
        def _():
            across(1)
            across(3)

        @pl.when(k == 1)
        def _():
            across(2)

        return 0

    lax.fori_loop(0, NZ, blocks1, 0)

    for h in range(HEADS):
        rl = 1.0 / ll[h]
        rd[h] = jnp.sum(gt[h].astype(f32) * (oo[h] * rl), axis=0, keepdims=True)
        ll[h] = rl
        dqt[h] = jnp.zeros((HD, RL), f32)

    def grads(base, n, h):
        s_ref[h % 2, 0:n, :] = dot(kv[pl.ds(base, n), HD : 2 * HD], gt[h])

    def gscores(slot, n, h, first):
        fac = jnp.exp2(m_ref[slot, h] - mm[h]) * ll[h]
        e = er_ref[:, hc(h)] if first else e_ref[slot, :, hc(h)]
        p = e.astype(f32) * fac
        pb = p.astype(bf16)
        if first:
            er_ref[:, hc(h)] = pb
        else:
            e_ref[slot, :, hc(h)] = pb
        gs_ref[0:n, hc(h)] = (p * (s_ref[h % 2, 0:n, :] - rd[h])).astype(bf16)

    def dqs(slot, n, h):
        dqt[h] += dot(kvt[slot, 0:HD, 0:n], gs_ref[0:n, hc(h)])

    def pass2(slot, base, n, first, heads=range(HEADS)):
        grads(base, n, heads[0])
        for h in heads:
            if h < heads[-1]:
                grads(base, n, h + 1)
            gscores(slot, n, h, first)
            if h > heads[0]:
                dqs(slot, n, h - 1)
        dqs(slot, n, heads[-1])

    def key_grads(slot, n, first):
        pb = er_ref[...] if first else e_ref[slot]
        gblk[0:n, 0:HD] = dot(gs_ref[0:n, :], qa[...]) * SCALE
        gblk[0:n, HD : 2 * HD] = dot(pb, ga[...])

    pass2(NX, NP, RL, True)
    key_grads(NX, RL, True)
    rg_all[tn] = gblk[0:RL, :].astype(bf16)

    def t_own(i):
        ref = rg_all.at[tn]
        return remote(ref, ref, t_s.at[i], t_r.at[i], dev_l if i == 0 else dev_y(i))

    def t_fwd(i):
        ref = rg_all.at[y * NL + 1 - lo]
        return remote(ref, ref, t_s.at[3 + i], t_r.at[3 + i], dev_y(i))

    for i in range(4):
        t_own(i).start()

    def rs_c(k):
        return remote(rcs.at[k], rcr.at[k], rc_s.at[k], rc_r.at[k], core)

    def rs_x(k, i):
        return remote(
            rxs.at[k, i], rxr.at[k, i], rx_s.at[k, i], rx_r.at[k, i], dev_x(offset(i + 1))
        )

    def rs_z(k):
        return remote(
            rzs.at[k], rzr.at[k], rz_s.at[k], rz_r.at[k], dev_z(NZ - offset(NZ - 1 - k))
        )

    def sum_core(k):
        rs_c(k).wait_recv()
        for i in (2, 0, 1):
            x2 = lax.rem(x + offset(i + 1), NX)
            rxs[k, i] = (keep[k, x2] + rcr[k, x2].astype(f32)).astype(bf16)
            rs_x(k, i).start()
        keep[k, x] = keep[k, x] + rcr[k, x].astype(f32)

    def sum_x(k):
        tot = keep[k, x]
        for i in range(NX - 1):
            rs_x(k, i).wait_recv()
            tot = tot + rxr[k, i].astype(f32)
        return tot

    def send_z(k):
        rzs[k] = sum_x(k).astype(bf16)
        rs_z(k).start()

    def blocks2(k, _):
        slot = NZ - 1 - k
        base = block_of(slot)
        pass2(slot, base, BLK, False, range(0, HEADS // 2))

        @pl.when(k > 0)
        def _():
            sum_core(k - 1)

        @pl.when(k > 1)
        def _():
            send_z(k - 2)

        pass2(slot, base, BLK, False, range(HEADS // 2, HEADS))
        key_grads(slot, BLK, False)
        for i in range(NX):
            rcs[k, i] = gblk[pl.ds(al((i * NC + oc) * PR, PR), PR), :].astype(bf16)
            keep[k, i] = gblk[pl.ds(al((i * NC + c) * PR, PR), PR), :]
        rs_c(k).start()

        @pl.when(k == 1)
        def _():
            t_own(0).wait_recv()
            for i in range(1, 4):
                t_fwd(i).start()

        return 0

    lax.fori_loop(0, NZ, blocks2, 0)
    sum_core(NZ - 1)

    for h in range(HEADS):
        dq_out[:, h * HD : (h + 1) * HD] = (dqt[h].T * SCALE).astype(bf16)
    out_dq = pltpu.make_async_copy(dq_out, dq_hbm.at[0], out_sem.at[0])
    out_dq.start()

    send_z(NZ - 2)

    for o in range(1, NT):
        w_send(o).wait_recv()
        w_core(o).start()
    wsl[tn] = w[pl.ds(al(tn * DT, DT), DT), :]
    pxt[...] = px[...].T
    rxt[...] = rx[...].T
    own_rg = rg_all[tn]
    for i in range(NX):
        rows = slice(i * (DM // NX), (i + 1) * (DM // NX))
        dwr[rows, :] = dot(rxt[rows, :], own_rg)

    tot = sum_x(NZ - 1)
    for i in range(3):
        rs_z(i).wait_recv()
        tot = tot + rzr[i].astype(f32)
    pg = tot.astype(bf16)
    pg_all[tn] = pg

    def p_send(o):
        return remote(pg_all.at[tn], pg_all.at[tn], p_s.at[o - 1], p_r.at[o - 1], dev_t(o))

    def dw_c(g):
        return remote(dcs.at[g], dcr.at[g], dc_s.at[g], dc_r.at[g], core)

    def dw_x(g, i):
        return remote(
            dxs.at[g, i], dxr.at[g, i], dx_s.at[g, i], dx_r.at[g, i], dev_x(offset(3 - i))
        )

    def dw_z(g):
        return remote(dzs.at[g], dzr.at[g], dz_s.at[g], dz_r.at[g], dev_z(offset(3 - g)))

    def dw_group(g, _):
        zz = lax.rem(z + offset(3 - g), NZ)
        for i in range(NX):
            xx = lax.rem(x + offset(3 - i), NX)
            first = (xx * NZ + zz) * NC
            theirs = pl.ds(al((first + oc) * DR, DR), DR)
            mine = pl.ds(al((first + c) * DR, DR), DR)
            dcs[g, i] = (dwr[theirs, :] + dot(pxt[theirs, :], pg)).astype(bf16)
            dkeep[g, i] = dwr[mine, :] + dot(pxt[mine, :], pg)
        dw_c(g).start()
        return 0

    lax.fori_loop(0, NZ, dw_group, 0)
    for o in range(1, NT):
        p_send(o).start()

    def dw_sum(g, _):
        dw_c(g).wait_recv()
        for i in range(NX - 1):
            dxs[g, i] = (dkeep[g, i] + dcr[g, i].astype(f32)).astype(bf16)
            dw_x(g, i).start()
        dkeep[g, NX - 1] = dkeep[g, NX - 1] + dcr[g, NX - 1].astype(f32)
        return 0

    lax.fori_loop(0, NZ, dw_sum, 0)

    for i in range(1, 4):
        t_own(i).wait_recv()
        t_fwd(i).wait_recv()
    for o in range(1, NT):
        w_core(o).wait_recv()
    acc = dot_t(rg_all[0], wsl[0])
    for t2 in range(1, NT):
        acc = acc + dot_t(rg_all[t2], wsl[t2])
    drx_out[...] = acc.astype(bf16)
    out_drx = pltpu.make_async_copy(drx_out, drx_hbm.at[0], out_sem.at[1])
    out_drx.start()

    def dw_last(g, _):
        for i in range(NX - 1):
            dw_x(g, i).wait_recv()
        tot = dkeep[g, NX - 1]
        for i in range(NX - 1):
            tot = tot + dxr[g, i].astype(f32)
        dkeep[g, NX - 1] = tot

        @pl.when(g < NZ - 1)
        def _():
            dzs[g] = tot.astype(bf16)
            dw_z(g).start()

        return 0

    lax.fori_loop(0, NZ, dw_last, 0)

    for o in range(1, NT):
        p_send(o).wait_recv()
    acc = dot_t(pg_all[0], wsl[0])
    for t2 in range(1, NT):
        acc = acc + dot_t(pg_all[t2], wsl[t2])
    dpx_out[...] = acc.astype(bf16)
    out_dpx = pltpu.make_async_copy(dpx_out, dpx_hbm, out_sem.at[2])
    out_dpx.start()

    for g in range(NZ - 1):
        dw_z(g).wait_recv()
    tot = dkeep[NZ - 1, NX - 1]
    for g in range(NZ - 1):
        tot = tot + dzr[g].astype(f32)
    dw_out[0] = tot[:, 0:HD].astype(bf16)
    dw_out[1] = tot[:, HD : 2 * HD].astype(bf16)
    out_dwk = pltpu.make_async_copy(dw_out.at[0], dwk_hbm, out_sem.at[3])
    out_dwv = pltpu.make_async_copy(dw_out.at[1], dwv_hbm, out_sem.at[4])
    out_dwk.start()
    out_dwv.start()

    for i in range(3):
        ag_z(i).wait_send()
        for j in range(NZ):
            ag_x(j, i).wait_send()
        rs_z(i).wait_send()
        dw_z(i).wait_send()
    for k in range(NX):
        for j in range(NZ):
            ag_c(k, j).wait_send()
        rs_c(k).wait_send()
        dw_c(k).wait_send()
        for i in range(NX - 1):
            rs_x(k, i).wait_send()
            dw_x(k, i).wait_send()
    for o in range(1, NT):
        w_send(o).wait_send()
        w_core(o).wait_send()
        p_send(o).wait_send()
    for i in range(4):
        t_own(i).wait_send()
    for i in range(1, 4):
        t_fwd(i).wait_send()
    for cp in (out_dq, out_drx, out_dpx, out_dwk, out_dwv):
        cp.wait()


def finish(*refs):
    n = len(refs) // 2
    for src, dst in zip(refs[:n], refs[n:]):
        dst[...] = src[...]


def local(prompt_x, resp_x, queries, d_attn, w_key, w_value, lengths):
    any_ = pl.BlockSpec(memory_space=pl.ANY)
    v = pltpu.VMEM
    dma = pltpu.SemaphoreType.DMA
    scratch = [
        v((PR, DM), bf16), v((RL, DM), bf16), v((RL, HEADS * HD), bf16), v((RL, HEADS * HD), bf16),
        v((DM, 2 * HD), bf16), v((DM, RL), bf16), v((DM, PR), bf16),
        v((NP + RL, 2 * HD), bf16), v((NX + 1, 2 * HD, BLK), bf16),
        v((HEADS * RL, HD), bf16), v((HEADS * RL, HD), bf16),
        v((HEADS, HD, RL), bf16), v((HEADS, HD, RL), bf16),
        v((NX, BLK, HEADS * RL), bf16), v((RL, HEADS * RL), bf16), v((BLK, HEADS * RL), bf16),
        v((2, BLK, RL), f32), v((2, 1, RL), f32), v((NX + 1, HEADS, 1, RL), f32),
        v((HEADS, 1, RL), f32), v((HEADS, 1, RL), f32), v((HEADS, HD, RL), f32),
        v((HEADS, 1, RL), f32), v((HEADS, 1, RL), f32), v((HEADS, 1, RL), f32),
        v((HEADS, HD, RL), f32),
        v((BLK, 2 * HD), f32), v((NZ, NX, PR, 2 * HD), f32),
        v((NZ, NX, PR, 2 * HD), bf16), v((NZ, NX, PR, 2 * HD), bf16),
        v((NZ, 3, PR, 2 * HD), bf16), v((NZ, 3, PR, 2 * HD), bf16),
        v((3, PR, 2 * HD), bf16), v((3, PR, 2 * HD), bf16),
        v((NT, RL, 2 * HD), bf16), v((NT, PR, 2 * HD), bf16), v((NT, DT, 2 * HD), bf16),
        v((DM, 2 * HD), f32), v((NZ, NX, DR, 2 * HD), f32),
        v((NZ, NX, DR, 2 * HD), bf16), v((NZ, NX, DR, 2 * HD), bf16),
        v((NZ, NX - 1, DR, 2 * HD), bf16), v((NZ, NX - 1, DR, 2 * HD), bf16),
        v((NZ - 1, DR, 2 * HD), bf16), v((NZ - 1, DR, 2 * HD), bf16),
        v((RL, HEADS * HD), bf16), v((RL, DT), bf16), v((PR, DT), bf16), v((2, DR, HD), bf16),
        dma((6,)), dma((5,)),
        dma((3,)), dma((3,)), dma((3, NZ)), dma((3, NZ)), dma((NX, NZ)), dma((NX, NZ)),
        dma((NT - 1,)), dma((NT - 1,)), dma((NT - 1,)), dma((NT - 1,)),
        dma((NT - 1,)), dma((NT - 1,)),
        dma((NZ,)), dma((NZ,)), dma((NZ, 3)), dma((NZ, 3)), dma((3,)), dma((3,)),
        dma((NT - 1,)), dma((NT - 1,)),
        dma((NZ,)), dma((NZ,)), dma((NZ, 3)), dma((NZ, 3)), dma((3,)), dma((3,)),
    ]
    shapes = (
        jax.ShapeDtypeStruct((1, RL, HEADS * HD), bf16),
        jax.ShapeDtypeStruct((1, RL, DT), bf16),
        jax.ShapeDtypeStruct((PR, DT), bf16),
        jax.ShapeDtypeStruct((DR, HD), bf16),
        jax.ShapeDtypeStruct((DR, HD), bf16),
    )
    outs = pl.pallas_call(
        kernel,
        out_shape=shapes,
        in_specs=[any_] * 6 + [pl.BlockSpec(memory_space=pltpu.SMEM)],
        out_specs=(any_,) * 5,
        scratch_shapes=scratch,
        compiler_params=pltpu.CompilerParams(
            collective_id=0, has_side_effects=True, vmem_limit_bytes=63 * 2**20
        ),
        name="kv_backward",
    )(prompt_x, resp_x, queries, d_attn, w_key, w_value, lengths)
    vmem = pl.BlockSpec(memory_space=pltpu.VMEM)
    return pl.pallas_call(
        finish,
        out_shape=shapes,
        in_specs=[vmem] * 5,
        out_specs=(vmem,) * 5,
        name="finish",
    )(*outs)


def solution(mesh):
    placed = (
        P("sample", None),
        P("sample", None, None),
        P("sample", None, "tensor"),
        P("sample", None, "tensor"),
        P(None, "tensor"),
        P(None, "tensor"),
        P("sample"),
    )
    return jax.shard_map(
        local,
        mesh=mesh,
        in_specs=placed,
        out_specs=(
            P("sample", None, "tensor"),
            P("sample", None, "tensor"),
            P("sample", "tensor"),
            P("sample", "tensor"),
            P("sample", "tensor"),
        ),
        check_vma=False,
    )
```

```python
import functools
import math

import jax
import jax.numpy as jnp
from jax import lax
from jax.experimental import pallas as pl
from jax.experimental.pallas import tpu as pltpu
from jax.sharding import PartitionSpec as P

f32 = jnp.float32
bf16 = jnp.bfloat16
MESH = pl.DeviceIdType.MESH
HD = 128
HEADS = 8
RL = 256
NX, NZ, NC, NY, NL = 4, 4, 2, 4, 2
NT = NY * NL
PR = 96
BLK = NX * NC * PR
NP = NZ * BLK
DM = 5120
DR = DM // (NX * NZ * NC)
DX = 128
DT = DM // NT
SCALE = HD**-0.5
SCALE2 = SCALE * math.log2(math.e)


def dot(a, b):
    return lax.dot_general(a, b, (((1,), (0,)), ((), ())), preferred_element_type=f32)


def dot_t(a, b):
    return lax.dot_general(a, b, (((1,), (1,)), ((), ())), preferred_element_type=f32)


def offset(k):
    return k + k // 2 - 2 * (k // 3)


def kernel(
    px_hbm, rx_hbm, q_hbm, g_hbm, wk_hbm, wv_hbm, len_ref,
    dq_hbm, drx_hbm, dpx_hbm, dwk_hbm, dwv_hbm,
    px, rx, q_in, g_in, w, rxt, pxt,
    kv, kvt, qa, ga, qt, gt,
    e_ref, er_ref, gs_ref, s_ref, mc_ref, m_ref, mm, ll, oo, al_ref, be_ref, rd, dqt,
    gblk, keep, rcs, rcr, rxs, rxr, rzs, rzr,
    rg_all, pg_all, pg2, wsl, dkeep, dcs, dcr, dxs, dxr, dzs, dzr,
    zfs, zfr, xfs, xfr, xkeep,
    dq_out, drx_out, dpx_out, dw_out,
    ld_sem, out_sem,
    agz_s, agz_r, agx_s, agx_r, agc_s, agc_r,
    w_s, w_r, wc_s, wc_r, pc_s, pc_r, t_s, t_r,
    rc_s, rc_r, rx_s, rx_r, rz_s, rz_r, p_s, p_r,
    dc_s, dc_r, dx_s, dx_r, dz_s, dz_r, zf_s, zf_r, xf_s, xf_r,
):
    sm = lax.axis_index("sample")
    tn = lax.axis_index("tensor")
    c = lax.rem(sm, NC)
    z = lax.rem(sm // NC, NZ)
    x = sm // (NC * NZ)
    y = tn // NL
    lo = lax.rem(tn, NL)
    oc = 1 - c

    def dev_s(xx, zz, cc):
        return ((xx * NZ + zz) * NC + cc, tn)

    core = dev_s(x, z, oc)

    def dev_x(o):
        return dev_s(lax.rem(x + o, NX), z, c)

    def dev_z(o):
        return dev_s(x, lax.rem(z + o, NZ), c)

    def dev_t(o):
        return (sm, lax.rem(tn + o, NT))

    def dev_y(o):
        return (sm, lax.rem(y + o, NY) * NL + lo)

    dev_l = (sm, y * NL + 1 - lo)

    def remote(src, dst, ss, rs, dev):
        return pltpu.make_async_remote_copy(
            src_ref=src, dst_ref=dst, send_sem=ss, recv_sem=rs, device_id=dev,
            device_id_type=MESH,
        )

    def al(v, n):
        return pl.multiple_of(v, n)

    own_rows = pl.ds(al(c * PR, PR), PR)
    loads = [
        pltpu.make_async_copy(px_hbm, px.at[own_rows, :], ld_sem.at[0]),
        pltpu.make_async_copy(wk_hbm, w.at[:, pl.ds(0, HD)], ld_sem.at[1]),
        pltpu.make_async_copy(wv_hbm, w.at[:, pl.ds(HD, HD)], ld_sem.at[2]),
        pltpu.make_async_copy(rx_hbm.at[0], rx, ld_sem.at[3]),
        pltpu.make_async_copy(q_hbm.at[0], q_in, ld_sem.at[4]),
        pltpu.make_async_copy(g_hbm.at[0], g_in, ld_sem.at[5]),
    ]
    for cp in loads:
        cp.start()

    barrier = pltpu.get_barrier_semaphore()
    peers = [core] + [dev_x(o) for o in (1, 2, 3)] + [dev_z(o) for o in (1, 2, 3)]
    peers += [dev_t(o) for o in range(1, NT)]
    for dev in peers:
        pl.semaphore_signal(barrier, inc=1, device_id=dev, device_id_type=MESH)

    loads[0].wait()
    loads[1].wait()
    loads[2].wait()

    def chunk(xx, zz, cc):
        return pl.ds(al(((zz * NX + xx) * NC + cc) * PR, PR), PR)

    kv[chunk(x, z, c), :] = dot(px[own_rows, :], w[...]).astype(bf16)
    pl.semaphore_wait(barrier, len(peers))

    def ag_z(i):
        rows = chunk(x, z, c)
        return remote(kv.at[rows, :], kv.at[rows, :], agz_s.at[i], agz_r.at[i], dev_z(i + 1))

    def ag_x(j, i):
        rows = chunk(x, lax.rem(z - j + NZ, NZ), c)
        return remote(
            kv.at[rows, :], kv.at[rows, :], agx_s.at[i, j], agx_r.at[i, j],
            dev_x(offset(i + 1)),
        )

    def ag_c(k, j):
        rows = chunk(lax.rem(x - offset(k) + NX, NX), lax.rem(z - j + NZ, NZ), c)
        return remote(kv.at[rows, :], kv.at[rows, :], agc_s.at[k, j], agc_r.at[k, j], core)

    for i in (1, 0, 2):
        ag_z(i).start()
    for i in (2, 0, 1):
        ag_x(0, i).start()
    ag_c(0, 0).start()

    def w_send(o):
        t2 = lax.rem(tn + o, NT)
        src = w.at[pl.ds(al(t2 * DT + c * (DT // 2), DT // 2), DT // 2), :]
        dst = wsl.at[tn, pl.ds(al(c * (DT // 2), DT // 2), DT // 2), :]
        return remote(src, dst, w_s.at[o - 1], w_r.at[o - 1], dev_t(o))

    def w_core(o):
        ref = wsl.at[
            lax.rem(tn - o + NT, NT), pl.ds(al(c * (DT // 2), DT // 2), DT // 2), :
        ]
        return remote(ref, ref, wc_s.at[o - 1], wc_r.at[o - 1], core)

    for o in (4, 2, 6):
        w_send(o).start()

    px_copy = remote(px.at[own_rows, :], px.at[own_rows, :], pc_s.at[0], pc_r.at[0], core)

    loads[3].wait()
    kv[NP : NP + RL, :] = dot(rx[...], w[...]).astype(bf16)
    loads[4].wait()
    loads[5].wait()
    valid = lax.broadcasted_iota(jnp.int32, (RL, HD), 0) < len_ref[0]
    for h in range(HEADS):
        qh = q_in[:, h * HD : (h + 1) * HD]
        gh = jnp.where(valid, g_in[:, h * HD : (h + 1) * HD], jnp.zeros((RL, HD), bf16))
        qa[h * RL : (h + 1) * RL, :] = qh
        ga[h * RL : (h + 1) * RL, :] = gh
        qt[h] = qh.T
        gt[h] = gh.T
    kvt[NX, :, 0:RL] = kv[NP : NP + RL, :].T

    def hc(h):
        return slice(h * RL, (h + 1) * RL)

    def scores(base, n, h, first):
        s = dot(kv[pl.ds(base, n), 0:HD], qt[h])
        if first:
            ri = lax.broadcasted_iota(jnp.int32, (RL, RL), 0)
            ci = lax.broadcasted_iota(jnp.int32, (RL, RL), 1)
            s = jnp.where(ri <= ci, s, -jnp.inf)
        s_ref[h % 2, 0:n, :] = s
        mc_ref[h % 2] = jnp.max(s, axis=0, keepdims=True) * SCALE2

    def expo(slot, n, h, first):
        mc = mc_ref[h % 2]
        e = jnp.exp2(s_ref[h % 2, 0:n, :] * SCALE2 - mc)
        lc = jnp.sum(e, axis=0, keepdims=True)
        if first:
            er_ref[:, hc(h)] = e.astype(bf16)
        else:
            e_ref[slot, :, hc(h)] = e.astype(bf16)
        m_ref[slot, h] = mc
        if first:
            mm[h] = mc
            ll[h] = lc
        else:
            mo = mm[h]
            mn = jnp.maximum(mo, mc)
            a = jnp.exp2(mo - mn)
            b = jnp.exp2(mc - mn)
            mm[h] = mn
            ll[h] = ll[h] * a + lc * b
            al_ref[h] = a
            be_ref[h] = b

    def outs(slot, n, h, first):
        e = er_ref[:, hc(h)] if first else e_ref[slot, :, hc(h)]
        o = dot(kvt[slot, HD : 2 * HD, 0:n], e)
        oo[h] = o if first else oo[h] * al_ref[h] + o * be_ref[h]

    def pass1(slot, base, n, first):
        scores(base, n, 0, first)
        for h in range(HEADS):
            if h < HEADS - 1:
                scores(base, n, h + 1, first)
            expo(slot, n, h, first)
            if h:
                outs(slot, n, h - 1, first)
        outs(slot, n, HEADS - 1, first)

    pass1(NX, NP, RL, True)

    def along_x(j):
        ag_z(j - 1).wait_recv()
        for i in (2, 0, 1):
            ag_x(j, i).start()
        ag_c(0, j).start()

    def across(j):
        for k in (1, 2, 3):
            ag_x(j, k - 1).wait_recv()
            ag_c(k, j).start()

    rxt[...] = rx[...].T
    along_x(1)
    along_x(3)
    across(0)
    along_x(2)
    for o in (3, 5, 1, 7):
        w_send(o).start()

    def block_of(k):
        return al(lax.rem(z - offset(k) + NZ, NZ) * BLK, BLK)

    def blocks1(k, _):
        for i in range(NX):
            ag_c(i, offset(k)).wait_recv()
        base = block_of(k)
        kvt[k] = kv[pl.ds(base, BLK), :].T
        pass1(k, base, BLK, False)

        @pl.when(k == 0)
        def _():
            across(1)
            across(3)

        @pl.when(k == 1)
        def _():
            across(2)

        return 0

    lax.fori_loop(0, NZ, blocks1, 0)

    px_copy.start()
    for h in range(HEADS):
        rl = 1.0 / ll[h]
        rd[h] = jnp.sum(gt[h].astype(f32) * (oo[h] * rl), axis=0, keepdims=True)
        ll[h] = rl

    def grads(base, n, h):
        s_ref[h % 2, 0:n, :] = dot(kv[pl.ds(base, n), HD : 2 * HD], gt[h])

    def gslot(slot):
        return (NZ - slot) // NZ if not isinstance(slot, int) else 0

    def gscores(slot, n, h, first):
        fac = jnp.exp2(m_ref[slot, h] - mm[h]) * ll[h]
        e = er_ref[:, hc(h)] if first else e_ref[slot, :, hc(h)]
        p = e.astype(f32) * fac
        pb = p.astype(bf16)
        if first:
            er_ref[:, hc(h)] = pb
        else:
            e_ref[slot, :, hc(h)] = pb
        gs_ref[gslot(slot), 0:n, hc(h)] = (p * (s_ref[h % 2, 0:n, :] - rd[h])).astype(bf16)

    def pass2(slot, base, n, first):
        grads(base, n, 0)
        for h in range(HEADS):
            if h < HEADS - 1:
                grads(base, n, h + 1)
            gscores(slot, n, h, first)

    def key_grads(slot, n, first):
        pb = er_ref[...] if first else e_ref[slot]
        gs = gs_ref[gslot(slot), 0:n, :]
        gblk[0:n, 0:HD] = dot(gs, qa[...]) * SCALE
        gblk[0:n, HD : 2 * HD] = dot(pb, ga[...])

    pass2(NX, NP, RL, True)
    key_grads(NX, RL, True)
    dqt[...] = dot(kvt[NX, 0:HD, 0:RL], gs_ref[0, 0:RL, :])
    rg_all[tn] = gblk[0:RL, :].astype(bf16)

    def t_own(i):
        ref = rg_all.at[tn]
        return remote(ref, ref, t_s.at[i], t_r.at[i], dev_l if i == 0 else dev_y(i))

    def t_fwd(i):
        ref = rg_all.at[y * NL + 1 - lo]
        return remote(ref, ref, t_s.at[3 + i], t_r.at[3 + i], dev_y(i))

    for i in range(4):
        t_own(i).start()

    def rs_c(k):
        return remote(rcs.at[k], rcr.at[k], rc_s.at[k], rc_r.at[k], core)

    def rs_x(k, i):
        return remote(
            rxs.at[k, i], rxr.at[k, i], rx_s.at[k, i], rx_r.at[k, i], dev_x(offset(i + 1))
        )

    def rs_z(k):
        return remote(
            rzs.at[k], rzr.at[k], rz_s.at[k], rz_r.at[k], dev_z(NZ - offset(NZ - 1 - k))
        )

    def sum_core(k):
        rs_c(k).wait_recv()
        for i in (2, 0, 1):
            x2 = lax.rem(x + offset(i + 1), NX)
            rxs[k, i] = (keep[k, x2] + rcr[k, x2].astype(f32)).astype(bf16)
            rs_x(k, i).start()
        keep[k, x] = keep[k, x] + rcr[k, x].astype(f32)

    def sum_x(k):
        tot = keep[k, x]
        for i in range(NX - 1):
            rs_x(k, i).wait_recv()
            tot = tot + rxr[k, i].astype(f32)
        return tot

    def send_z(k):
        rzs[k] = sum_x(k).astype(bf16)
        rs_z(k).start()

    def blocks2(k, _):
        slot = NZ - 1 - k
        base = block_of(slot)
        pass2(slot, base, BLK, False)

        @pl.when(k > 0)
        def _():
            sum_core(k - 1)

        @pl.when(k > 1)
        def _():
            send_z(k - 2)

        @pl.when(k == 1)
        def _():
            for o in range(1, NT):
                w_send(o).wait_recv()
                w_core(o).start()

        key_grads(slot, BLK, False)

        @pl.when(k < NZ - 2)
        def _():
            dqt[...] += dot(kvt[slot, 0:HD, :], gs_ref[0])

        for i in range(NX):
            rcs[k, i] = gblk[pl.ds(al((i * NC + oc) * PR, PR), PR), :].astype(bf16)
            keep[k, i] = gblk[pl.ds(al((i * NC + c) * PR, PR), PR), :]
        rs_c(k).start()

        @pl.when(k == 1)
        def _():
            t_own(0).wait_recv()
            for i in range(1, 4):
                t_fwd(i).start()

        return 0

    lax.fori_loop(0, NZ, blocks2, 0)

    def dw_c(g):
        return remote(dcs.at[g], dcr.at[g], dc_s.at[g], dc_r.at[g], core)

    def dw_x(g, i):
        return remote(
            dxs.at[g, i], dxr.at[g, i], dx_s.at[g, i], dx_r.at[g, i], dev_x(offset(3 - i))
        )

    def dw_z(g):
        return remote(dzs.at[g], dzr.at[g], dz_s.at[g], dz_r.at[g], dev_z(offset(3 - g)))

    def zf(g):
        return remote(zfs.at[g], zfr.at[g], zf_s.at[g], zf_r.at[g], dev_z(offset(3 - g)))

    def xf(i):
        return remote(xfs.at[i], xfr.at[i], xf_s.at[i], xf_r.at[i], dev_x(offset(3 - i)))

    def dw_rows(g, i, cc):
        zz = lax.rem(z + offset(3 - g), NZ)
        xx = lax.rem(x + offset(3 - i), NX)
        return pl.ds(al(((xx * NZ + zz) * NC + cc) * DR, DR), DR)

    own_rg = rg_all[tn]

    def dw_resp(g, _):
        for i in range(NX):
            dcs[g, i] = dot(rxt[dw_rows(g, i, oc), :], own_rg).astype(bf16)
            dkeep[g, i] = dot(rxt[dw_rows(g, i, c), :], own_rg)
        dw_c(g).start()
        return 0

    lax.fori_loop(0, NZ, dw_resp, 0)
    sum_core(NZ - 1)
    send_z(NZ - 2)
    px_copy.wait_recv()
    pxt[...] = px[...].T

    def dw_both(g, _):
        dw_c(g).wait_recv()
        for i in range(NX):
            dkeep[g, i] = dkeep[g, i] + dcr[g, i].astype(f32)
        return 0

    lax.fori_loop(0, NZ, dw_both, 0)

    tot = sum_x(NZ - 1)
    for i in range(3):
        rs_z(i).wait_recv()
        tot = tot + rzr[i].astype(f32)
    pg = tot.astype(bf16)
    pg_all[tn] = pg

    def p_send(o):
        return remote(pg_all.at[tn], pg_all.at[tn], p_s.at[o - 1], p_r.at[o - 1], dev_t(o))

    pg2[own_rows, :] = pg
    pg_copy = remote(pg2.at[own_rows, :], pg2.at[own_rows, :], pc_s.at[1], pc_r.at[1], core)
    pg_copy.start()
    for o in range(1, NT):
        p_send(o).start()
    pg_copy.wait_recv()
    pg_both = pg2[...]

    def dw_sum(g, _):
        for i in range(NX):
            tot = dkeep[g, i] + dot(pxt[dw_rows(g, i, c), :], pg_both)
            dkeep[g, i] = tot
            if i < NX - 1:
                dxs[g, i] = tot[0:DX].astype(bf16)
                dw_x(g, i).start()

        @pl.when(g < NZ - 1)
        def _():
            for i in range(NX):
                zfs[g, i] = dkeep[g, i, DX:DR, :].astype(bf16)
            zf(g).start()

        return 0

    lax.fori_loop(0, NZ, dw_sum, 0)

    for k in range(2):
        dqt[...] += dot(kvt[k, 0:HD, :], gs_ref[1 - k])
    for h in range(HEADS):
        dq_out[:, h * HD : (h + 1) * HD] = (dqt[:, hc(h)].T * SCALE).astype(bf16)
    out_dq = pltpu.make_async_copy(dq_out, dq_hbm.at[0], out_sem.at[0])
    out_dq.start()

    for g in range(NZ - 1):
        zf(g).wait_recv()
    for i in range(NX):
        tot = dkeep[NZ - 1, i, DX:DR, :]
        for g in range(NZ - 1):
            tot = tot + zfr[g, i].astype(f32)
        if i < NX - 1:
            xfs[i] = tot.astype(bf16)
            xf(i).start()
        else:
            xkeep[...] = tot

    for i in range(1, 4):
        t_own(i).wait_recv()
        t_fwd(i).wait_recv()
    for o in range(1, NT):
        w_core(o).wait_recv()
    wsl[tn] = w[pl.ds(al(tn * DT, DT), DT), :]
    acc = dot_t(rg_all[0], wsl[0])
    for t2 in range(1, NT):
        acc = acc + dot_t(rg_all[t2], wsl[t2])
    drx_out[...] = acc.astype(bf16)
    out_drx = pltpu.make_async_copy(drx_out, drx_hbm.at[0], out_sem.at[1])
    out_drx.start()

    def dw_last(g, _):
        for i in range(NX - 1):
            dw_x(g, i).wait_recv()
        tot = dkeep[g, NX - 1, 0:DX, :]
        for i in range(NX - 1):
            tot = tot + dxr[g, i].astype(f32)
        dkeep[g, NX - 1, 0:DX, :] = tot

        @pl.when(g < NZ - 1)
        def _():
            dzs[g] = tot.astype(bf16)
            dw_z(g).start()

        return 0

    lax.fori_loop(0, NZ, dw_last, 0)

    for o in range(1, NT):
        p_send(o).wait_recv()
    acc = dot_t(pg_all[0], wsl[0])
    for t2 in range(1, NT):
        acc = acc + dot_t(pg_all[t2], wsl[t2])
    dpx_out[...] = acc.astype(bf16)
    out_dpx = pltpu.make_async_copy(dpx_out, dpx_hbm, out_sem.at[2])
    out_dpx.start()

    for g in range(NZ - 1):
        dw_z(g).wait_recv()
    tot = dkeep[NZ - 1, NX - 1, 0:DX, :]
    for g in range(NZ - 1):
        tot = tot + dzr[g].astype(f32)
    dw_out[0, 0:DX, :] = tot[:, 0:HD].astype(bf16)
    dw_out[1, 0:DX, :] = tot[:, HD : 2 * HD].astype(bf16)
    tot = xkeep[...]
    for i in range(NX - 1):
        xf(i).wait_recv()
        tot = tot + xfr[i].astype(f32)
    dw_out[0, DX:DR, :] = tot[:, 0:HD].astype(bf16)
    dw_out[1, DX:DR, :] = tot[:, HD : 2 * HD].astype(bf16)
    out_dwk = pltpu.make_async_copy(dw_out.at[0], dwk_hbm, out_sem.at[3])
    out_dwv = pltpu.make_async_copy(dw_out.at[1], dwv_hbm, out_sem.at[4])
    out_dwk.start()
    out_dwv.start()

    for i in range(3):
        ag_z(i).wait_send()
        for j in range(NZ):
            ag_x(j, i).wait_send()
        rs_z(i).wait_send()
        dw_z(i).wait_send()
        zf(i).wait_send()
        xf(i).wait_send()
    for k in range(NX):
        for j in range(NZ):
            ag_c(k, j).wait_send()
        rs_c(k).wait_send()
        dw_c(k).wait_send()
        for i in range(NX - 1):
            rs_x(k, i).wait_send()
            dw_x(k, i).wait_send()
    for o in range(1, NT):
        w_send(o).wait_send()
        w_core(o).wait_send()
        p_send(o).wait_send()
    px_copy.wait_send()
    pg_copy.wait_send()
    for i in range(4):
        t_own(i).wait_send()
    for i in range(1, 4):
        t_fwd(i).wait_send()
    for cp in (out_dq, out_drx, out_dpx, out_dwk, out_dwv):
        cp.wait()


def finish(*refs):
    n = len(refs) // 2
    for src, dst in zip(refs[:n], refs[n:]):
        dst[...] = src[...]


def local(prompt_x, resp_x, queries, d_attn, w_key, w_value, lengths):
    any_ = pl.BlockSpec(memory_space=pl.ANY)
    v = pltpu.VMEM
    dma = pltpu.SemaphoreType.DMA
    scratch = [
        v((NC * PR, DM), bf16), v((RL, DM), bf16), v((RL, HEADS * HD), bf16), v((RL, HEADS * HD), bf16),
        v((DM, 2 * HD), bf16), v((DM, RL), bf16), v((DM, NC * PR), bf16),
        v((NP + RL, 2 * HD), bf16), v((NX + 1, 2 * HD, BLK), bf16),
        v((HEADS * RL, HD), bf16), v((HEADS * RL, HD), bf16),
        v((HEADS, HD, RL), bf16), v((HEADS, HD, RL), bf16),
        v((NZ, BLK, HEADS * RL), bf16), v((RL, HEADS * RL), bf16),
        v((2, BLK, HEADS * RL), bf16),
        v((2, BLK, RL), f32), v((2, 1, RL), f32), v((NX + 1, HEADS, 1, RL), f32),
        v((HEADS, 1, RL), f32), v((HEADS, 1, RL), f32), v((HEADS, HD, RL), f32),
        v((HEADS, 1, RL), f32), v((HEADS, 1, RL), f32), v((HEADS, 1, RL), f32),
        v((HD, HEADS * RL), f32),
        v((BLK, 2 * HD), f32), v((NZ, NX, PR, 2 * HD), f32),
        v((NZ, NX, PR, 2 * HD), bf16), v((NZ, NX, PR, 2 * HD), bf16),
        v((NZ, 3, PR, 2 * HD), bf16), v((NZ, 3, PR, 2 * HD), bf16),
        v((3, PR, 2 * HD), bf16), v((3, PR, 2 * HD), bf16),
        v((NT, RL, 2 * HD), bf16), v((NT, PR, 2 * HD), bf16), v((NC * PR, 2 * HD), bf16),
        v((NT, DT, 2 * HD), bf16), v((NZ, NX, DR, 2 * HD), f32),
        v((NZ, NX, DR, 2 * HD), bf16), v((NZ, NX, DR, 2 * HD), bf16),
        v((NZ, NX - 1, DX, 2 * HD), bf16), v((NZ, NX - 1, DX, 2 * HD), bf16),
        v((NZ - 1, DX, 2 * HD), bf16), v((NZ - 1, DX, 2 * HD), bf16),
        v((NZ - 1, NX, DR - DX, 2 * HD), bf16), v((NZ - 1, NX, DR - DX, 2 * HD), bf16),
        v((NX - 1, DR - DX, 2 * HD), bf16), v((NX - 1, DR - DX, 2 * HD), bf16),
        v((DR - DX, 2 * HD), f32),
        v((RL, HEADS * HD), bf16), v((RL, DT), bf16), v((PR, DT), bf16), v((2, DR, HD), bf16),
        dma((6,)), dma((5,)),
        dma((3,)), dma((3,)), dma((3, NZ)), dma((3, NZ)), dma((NX, NZ)), dma((NX, NZ)),
        dma((NT - 1,)), dma((NT - 1,)), dma((NT - 1,)), dma((NT - 1,)), dma((2,)), dma((2,)),
        dma((NT - 1,)), dma((NT - 1,)),
        dma((NZ,)), dma((NZ,)), dma((NZ, 3)), dma((NZ, 3)), dma((3,)), dma((3,)),
        dma((NT - 1,)), dma((NT - 1,)),
        dma((NZ,)), dma((NZ,)), dma((NZ, 3)), dma((NZ, 3)), dma((3,)), dma((3,)),
        dma((3,)), dma((3,)), dma((3,)), dma((3,)),
    ]
    shapes = (
        jax.ShapeDtypeStruct((1, RL, HEADS * HD), bf16),
        jax.ShapeDtypeStruct((1, RL, DT), bf16),
        jax.ShapeDtypeStruct((PR, DT), bf16),
        jax.ShapeDtypeStruct((DR, HD), bf16),
        jax.ShapeDtypeStruct((DR, HD), bf16),
    )
    outs = pl.pallas_call(
        kernel,
        out_shape=shapes,
        in_specs=[any_] * 6 + [pl.BlockSpec(memory_space=pltpu.SMEM)],
        out_specs=(any_,) * 5,
        scratch_shapes=scratch,
        compiler_params=pltpu.CompilerParams(
            collective_id=0, has_side_effects=True, vmem_limit_bytes=63 * 2**20
        ),
        name="kv_backward",
    )(prompt_x, resp_x, queries, d_attn, w_key, w_value, lengths)
    vmem = pl.BlockSpec(memory_space=pltpu.VMEM)
    return pl.pallas_call(
        finish,
        out_shape=shapes,
        in_specs=[vmem] * 5,
        out_specs=(vmem,) * 5,
        name="finish",
    )(*outs)


def solution(mesh):
    placed = (
        P("sample", None),
        P("sample", None, None),
        P("sample", None, "tensor"),
        P("sample", None, "tensor"),
        P(None, "tensor"),
        P(None, "tensor"),
        P("sample"),
    )
    return jax.shard_map(
        local,
        mesh=mesh,
        in_specs=placed,
        out_specs=(
            P("sample", None, "tensor"),
            P("sample", None, "tensor"),
            P("sample", "tensor"),
            P("sample", "tensor"),
            P("sample", "tensor"),
        ),
        check_vma=False,
    )
```
